32 devices in a mesh: frame: 4 (over x, core), row: 4 (over z), col: 2 (over y).
Axes of the slice: x: 2, y: 2, z: 4, core: 2. Of those that a mesh axis runs over, the one named last changes fastest.
Arguments:
- queries: bfloat16 [8, 32, 16, 2240], P('frame', 'row', 'col'), may hold values from -5 to 5
- keys: bfloat16 [8, 32, 16, 2240], P('frame', 'row', 'col'), may hold values from -120 to 120
- values: bfloat16 [8, 32, 16, 2240], P('frame', 'row', 'col'), may hold values from -12 to 12
- hidden: bfloat16 [8, 32, 16, 5632], P('frame', 'row', 'col'), may hold values from -5 to 5
- conv_weight: float32 [9, 5632], replicated, may hold values from -2 to 2
- conv_bias: float32 [5632], replicated, may hold values from -2.5 to 2.5
Outputs:
- attended: bfloat16 [8, 32, 16, 2240], P('frame', 'row', 'col')
- gated: bfloat16 [8, 32, 16, 2816], P('frame', 'row', 'col')
The draws below stay inside these ranges and needn't reach their ends.
All inputs are finite; a program needn't handle non-finite values.
Results may differ from the reference program's by a relative error of at most 0.0004.
Values may be sent and summed in bfloat16 or wider, within the bound.
No kernel may reach another device: no remote copies, remote signals or barrier semaphores. Data moves between devices by JAX's collectives and lax.ppermute only.
A program may use at most 64 MiB of HBM per device.

```python
import math
import jax
import jax.numpy as jnp
from jax import lax

HEADS = 70
HD = 32
HU = 2816
WIDTH = 2240
CONV_CH = 5632
FRAMES = 8
ROWS = 32
COLS = 16
N_FRAME = 4


def draw_keys(key, part):
    key = jax.random.fold_in(key, 11)
    first, second, third = jax.random.split(key, 3)
    base = jnp.clip(jax.random.normal(first, (FRAMES, ROWS, COLS, HEADS * HD), jnp.float32), -4.0, 4.0)
    top = math.log(10.0)
    scale = jnp.exp(jax.random.uniform(second, (FRAMES, ROWS, COLS, 1), jnp.float32, 0.0, top))
    region = jax.random.uniform(third, (FRAMES, (ROWS + 3) // 4, (COLS + 3) // 4, HEADS * HD), jnp.float32, 0.0, math.log(1000.0))
    region = jnp.repeat(jnp.repeat(region, 4, axis=1), 4, axis=2)[:, :ROWS, :COLS]
    return (base * scale * jnp.exp(-region)).astype(jnp.bfloat16)


def draw_values(key, part):
    key = jax.random.fold_in(key, 23)
    k_noise, k_frame, k_region, k_channel = jax.random.split(key, 4)
    shape = (FRAMES, ROWS, COLS, HEADS * HD)
    noise = 0.5 * jnp.clip(jax.random.normal(k_noise, shape, jnp.float32), -3.0, 3.0)
    frame_part = jnp.clip(jax.random.normal(k_frame, (FRAMES, 1, 1, HEADS * HD), jnp.float32), -3.0, 3.0)
    coarse = jnp.clip(jax.random.normal(k_region, (FRAMES, (ROWS + 3) // 4, (COLS + 3) // 4, HEADS * HD), jnp.float32), -3.0, 3.0)
    coarse = jnp.repeat(jnp.repeat(coarse, 4, axis=1), 4, axis=2)[:, :ROWS, :COLS]
    channel = jnp.clip(jax.random.normal(k_channel, (1, 1, 1, HEADS * HD), jnp.float32), -3.0, 3.0)
    return (noise + frame_part + 1.5 * coarse + channel).astype(jnp.bfloat16)


def level_of(stream_key, extent, pieces, least, top_value):
    def one(dim, blocks):
        steps = jax.random.uniform(jax.random.fold_in(jax.random.fold_in(stream_key, 6), dim), (blocks,), jnp.float32, least / len(pieces), top_value / len(pieces))
        return jnp.repeat(jnp.exp(steps), extent[dim] // blocks).reshape((-1,) + (1,) * (len(extent) - dim - 1))

    level = one(*pieces[0])
    for cut in pieces[1:]:
        level = level * one(*cut)
    return level


def scatter_about(rng, dims, spread, most, pieces=(), dtype=jnp.bfloat16):
    gain = level_of(rng, dims, pieces, -0.22, 0.18) if pieces else 1.0
    entries = jax.random.normal(rng, dims, jnp.float32) * spread * gain
    return jnp.minimum(jnp.maximum(entries, -most), most).astype(dtype)


def setup_inputs(seed: int = 0) -> dict:
    key_of = jax.random.split(jax.random.key(seed), 7)
    return {
        "queries": scatter_about(key_of[0], (FRAMES, ROWS, COLS, WIDTH), 1.0, 5.0, ((0, 4), (1, 4), (2, 2))),
        "keys": draw_keys(jax.random.fold_in(key_of[6], 71), 0),
        "values": draw_values(jax.random.fold_in(key_of[6], 71), 0),
        "hidden": scatter_about(key_of[3], (FRAMES, ROWS, COLS, CONV_CH), 1.0, 5.0, ((0, 4), (1, 4), (2, 2))),
        "conv_weight": scatter_about(key_of[4], (9, CONV_CH), 9 ** -0.5, 2.0, (), jnp.float32),
        "conv_bias": scatter_about(key_of[5], (CONV_CH,), 0.5, 2.5, (), jnp.float32),
    }


EPS = 1e-6
HIGH = lax.Precision.HIGHEST


def block_state(pair):
    key_block, value_block = pair
    kpos = jnp.maximum(key_block.astype(jnp.float32), 0.0).reshape(-1, HEADS, HD)
    vals = value_block.astype(jnp.float32).reshape(-1, HEADS, HD)
    state = jnp.einsum('thd,the->hde', kpos, vals, precision=HIGH)
    return state, jnp.sum(kpos, axis=0)


def block_output(triple):
    query_block, prefix, zprefix = triple
    qpos = jnp.maximum(query_block.astype(jnp.float32), 0.0).reshape(-1, HEADS, HD)
    numer = jnp.einsum('thd,hde->the', qpos, prefix, precision=HIGH)
    denom = jnp.einsum('thd,hd->th', qpos, zprefix, precision=HIGH) + EPS
    return (numer / denom[..., None]).reshape(-1, WIDTH).astype(jnp.bfloat16)


def reference(queries, keys, values, hidden, conv_weight, conv_bias):
    key_blocks = keys.reshape(N_FRAME, -1, WIDTH)
    value_blocks = values.reshape(N_FRAME, -1, WIDTH)
    query_blocks = queries.reshape(N_FRAME, -1, WIDTH)
    states, ksums = lax.map(block_state, (key_blocks, value_blocks))
    prefix = jnp.cumsum(states, axis=0)
    zprefix = jnp.cumsum(ksums, axis=0)
    attended = lax.map(block_output, (query_blocks, prefix, zprefix)).reshape(FRAMES, ROWS, COLS, WIDTH)

    def conv_frame(frame):
        padded = jnp.pad(frame.astype(jnp.float32), ((1, 1), (1, 1), (0, 0)))
        total = jnp.zeros((ROWS, COLS, CONV_CH), jnp.float32) + conv_bias
        for shift_r in range(3):
            for shift_c in range(3):
                total = total + conv_weight[3 * shift_r + shift_c] * padded[shift_r:shift_r + ROWS, shift_c:shift_c + COLS]
        return (total[..., :HU] * jax.nn.silu(total[..., HU:])).astype(jnp.bfloat16)

    gated = lax.map(conv_frame, hidden)
    return attended, gated
```

```python
import functools

import jax
import jax.numpy as jnp
from jax import lax
from jax.experimental import pallas as pl
from jax.experimental.pallas import tpu as pltpu
from jax.sharding import PartitionSpec as P

HEADS = 70
HD = 32
EPS = 1e-06
LANE = 128
F32 = jnp.float32
BF16 = jnp.bfloat16
VMEM_LIMIT = 40 * 1024 * 1024
VMEM_MOST = 60 * 1024 * 1024


def whole(n):
    return [pl.BlockSpec(memory_space=pltpu.VMEM)] * n


def lane_tiles(width):
    return -(-width // LANE)


def piece_rows(width, pieces):
    return 8 * -(-lane_tiles(width) * (HD + 1) // (8 * pieces))


def target(place, step, n):
    return place ^ step if n & (n - 1) == 0 else (place + step) % n


def source(place, step, n):
    return place ^ step if n & (n - 1) == 0 else (place + n - step) % n


def piece(place, per):
    return pl.ds(pl.multiple_of(place * per, 8), per)


def same_head(shape):
    first = lax.broadcasted_iota(jnp.int32, shape, 0) // HD
    second = lax.broadcasted_iota(jnp.int32, shape, 1) // HD
    return first == second


def state_kernel(width, pieces, keys, values, *refs):
    *outs, k_ref, v_ref, held, sems = refs
    tokens = k_ref.shape[0]
    tiles = lane_tiles(width)
    half = tiles // 2
    loads = []
    for c, (lo, hi) in enumerate(((0, half * LANE), (half * LANE, width))):
        at = pl.ds(lo, hi - lo)
        for i, (array, ref) in enumerate(((keys, k_ref), (values, v_ref))):
            loads.append(pltpu.make_async_copy(array.at[:, at], ref.at[:, at], sems.at[c, i]))
            loads[-1].start()
    ones = jnp.ones((8, tokens), BF16)
    held[tiles * HD :, :] = jnp.zeros((held.shape[0] - tiles * HD, LANE), F32)
    for j in range(tiles):
        if j in (0, half):
            for copy in loads[2 * (j // half) : 2 * (j // half) + 2]:
                copy.wait()
        lo, hi = j * LANE, min(width, (j + 1) * LANE)
        n = hi - lo
        kpos = jnp.maximum(k_ref[:, lo:hi], 0)
        vals = v_ref[:, lo:hi]
        full = lax.dot_general(kpos, vals, (((0,), (0,)), ((), ())), preferred_element_type=F32)
        ksum = jnp.dot(ones, kpos, preferred_element_type=F32)
        head = lax.broadcasted_iota(jnp.int32, (HD, n), 1) // HD
        packed = jnp.zeros((HD, n), F32)
        for i in range(n // HD):
            packed = jnp.where(head == i, full[i * HD : (i + 1) * HD, :], packed)
        if n < LANE:
            held[j * HD : (j + 1) * HD, :] = jnp.zeros((HD, LANE), F32)
        held[j * HD : (j + 1) * HD, :n] = packed
        held[tiles * HD + j : tiles * HD + j + 1, :n] = ksum[:1]
    mine = lax.axis_index(GROUP)
    for step, out in enumerate(outs):
        rows = piece(target(mine, step, pieces), 8 * out.shape[0])
        out[...] = held[rows, :].reshape(out.shape)


def halves(x):
    high = x.astype(BF16)
    return high, (x - high.astype(F32)).astype(BF16)


def attend_kernel(width, q_ref, *refs):
    *quarters, out, p_ref, out_ref, sems = refs
    mine, pieces = lax.axis_index(GROUP), len(quarters)
    for step, quarter in enumerate(quarters):
        rows = piece(source(mine, step, pieces), 8 * quarter.shape[0])
        p_ref[rows, :] = quarter[...].reshape(-1, LANE)
    tiles = lane_tiles(width)
    parts = sems.shape[0]
    firsts = [tiles * c // parts for c in range(parts + 1)]
    stores = []
    for j in range(tiles):
        lo, hi = j * LANE, min(width, (j + 1) * LANE)
        n = hi - lo
        qpos = jnp.maximum(q_ref[:, lo:hi], 0)
        same = same_head((n, n))
        part = p_ref[j * HD : (j + 1) * HD, :n]
        spread = jnp.where(same, jnp.concatenate([part] * (n // HD), axis=0), 0.0)
        zrow = p_ref[tiles * HD + j : tiles * HD + j + 1, :n]
        block = same.astype(F32).astype(BF16)
        numer = jnp.dot(
            jnp.concatenate([qpos, qpos], axis=1),
            jnp.concatenate(halves(spread), axis=0),
            preferred_element_type=F32,
        )
        denom = jnp.dot(
            jnp.concatenate(halves(qpos.astype(F32) * zrow), axis=1),
            jnp.concatenate([block, block], axis=0),
            preferred_element_type=F32,
        )
        out_ref[:, lo:hi] = (numer / (denom + EPS)).astype(BF16)
        if j + 1 in firsts:
            c = firsts.index(j + 1) - 1
            at = pl.ds(firsts[c] * LANE, hi - firsts[c] * LANE)
            stores.append(pltpu.make_async_copy(out_ref.at[:, at], out.at[:, at], sems.at[c]))
            stores[-1].start()
    for copy in stores:
        copy.wait()


def place(axis):
    return lax.axis_index(axis), lax.axis_size(axis)


def chosen(by_even, by_odd, mine, n):
    if n == 1:
        return jnp.zeros_like(by_even), jnp.zeros_like(by_even)
    if n == 2:
        return jnp.where(mine == 1, by_even, 0), jnp.where(mine == 0, by_even, 0)
    is_even = lax.rem(mine, 2) == 0
    before = jnp.where(is_even, by_odd, by_even)
    after = jnp.where(is_even, by_even, by_odd)
    return jnp.where(mine == 0, 0, before), jnp.where(mine == n - 1, 0, after)


def conv_kernel(hidden, row_e, row_o, col_e, col_o, weight, bias, out, held, sems):
    frames, rows, cols, channels = hidden.shape
    half = channels // 2
    in_rows, (col, n_cols) = place(ROW), place("col")
    steps, parts = half // LANE, sems.shape[0]

    def conv(f, i):
        at = pl.ds(pl.multiple_of(i * LANE, LANE), LANE)
        w = weight[:, at]
        spot = lax.broadcasted_iota(jnp.int32, (cols, LANE), 0)

        def part(ref):
            return ref[f, :, at].astype(F32)

        def column(edge, top, end):
            return jnp.concatenate([top, edge, end], axis=0)

        def corners(side):
            tiles = channels // LANE
            wide = -(-tiles // cols)
            first = channels + (side * wide + lax.rem(i, wide)) * LANE
            lanes = pl.ds(pl.multiple_of(first, LANE), LANE)
            both_lines = chosen(
                row_e[f, :, lanes].astype(F32), row_o[f, :, lanes].astype(F32), *in_rows
            )
            return [pltpu.roll(x, lax.rem(cols - i // wide, cols), 0)[:1] for x in both_lines]

        def taps(b):
            return [w[3 * a + b : 3 * a + b + 1] for a in range(3)]

        def along(taps, z):
            return sum(tap * z[a : a + rows] for a, tap in enumerate(taps))

        up, down = chosen(part(row_e), part(row_o), *in_rows)
        x = jnp.concatenate([up[None], hidden[f, :, :, at].astype(F32), down[None]], axis=0)
        total = along([tap[None] for tap in taps(1)], x) + bias[pl.ds(i, 1), :][None]
        for b, shift, edge in ((0, 1, 0), (2, cols - 1, cols - 1)):
            inside = [jnp.where(spot == edge, 0.0, tap)[None] for tap in taps(b)]
            total = total + along(inside, pltpu.roll(x, shift, 1))
        if n_cols == 2:
            sides = [jnp.where(col == 0, right, left) for left, right in zip(taps(0), taps(2))]
            beside = column(part(col_e), *corners(0))
            terms = [(jnp.where(col == 0, cols - 1, 0), along(sides, beside))]
        else:
            edges = chosen(part(col_e), part(col_o), col, n_cols)
            terms = [
                (border, along(taps(b), column(edge, *corners(side))))
                for side, (border, b, edge) in enumerate(zip((0, cols - 1), (0, 2), edges))
                if n_cols > 1
            ]
        for edge, term in terms:
            total = total + jnp.where((spot == edge)[None], term[:, None, :], 0.0)
        return total

    def tile(i, carry):
        first = pl.multiple_of(i * LANE, LANE)
        for f in range(frames):
            value, gate = conv(f, i), conv(f, i + steps)
            held[f, :, :, pl.ds(first, LANE)] = (
                0.5 * value * gate * (1.0 + jnp.tanh(0.5 * gate))
            ).astype(BF16)
        return carry

    stores = []
    for part in range(parts):
        lo, hi = steps * part // parts, steps * (part + 1) // parts
        lax.fori_loop(lo, hi, tile, 0)
        at = pl.ds(lo * LANE, (hi - lo) * LANE)
        for f in range(frames):
            stores.append(
                pltpu.make_async_copy(
                    held.at[f, :, :, at], out.at[f, :, :, at], sems.at[part, f]
                )
            )
            stores[-1].start()
    for copy in stores:
        copy.wait()


def swaps(n):
    even = [min(i ^ 1, n - 1) for i in range(n)]
    odd = [min(max(((i - 1) ^ 1) + 1, 0), n - 1) for i in range(n)]
    return [list(enumerate(to)) for to in ((even, odd) if n > 2 else (even,))]


def sends(first, last, axis):
    is_even = lax.rem(lax.axis_index(axis), 2) == 0
    return jnp.where(is_even, last, first), jnp.where(is_even, first, last)


def halo_sends(hidden):
    rows, cols = hidden.shape[1:3]
    to_rows = sends(hidden[:, 0], hidden[:, rows - 1], ROW)
    return to_rows, sends(hidden[:, :, 0], hidden[:, :, cols - 1], "col")


def with_corners(to_rows, by_cols):
    frames, cols, channels = to_rows[0].shape
    n_cols = lax.axis_size("col")
    if n_cols == 1:
        return to_rows
    sides = by_cols[:1] if n_cols == 2 else chosen(*by_cols, *place("col"))
    wide = -(-channels // (cols * LANE)) * LANE
    packed = []
    for side in sides:
        corners = sends(side[:, 0], side[:, side.shape[1] - 1], ROW)
        spare = ((0, 0), (0, cols * wide - channels))
        packed.append([jnp.pad(x, spare).reshape(frames, cols, wide) for x in corners])
    return [jnp.concatenate(parts, axis=2) for parts in zip(to_rows, *packed)]


def both(results):
    return [results[0], results[-1]]


def swap_even_rows(to_even):
    return lax.ppermute(to_even, ROW, swaps(lax.axis_size(ROW))[0])


def swap_odd_rows(to_odd):
    pairs = swaps(lax.axis_size(ROW))[1:]
    return lax.ppermute(to_odd, ROW, pairs[0]) if pairs else to_odd


def swap_columns(to_cols):
    pairs = swaps(lax.axis_size("col"))
    return both([lax.ppermute(x, "col", p) for x, p in zip(to_cols, pairs)])


def convolve(hidden, around, weight, bias):
    frames, rows, cols, channels = hidden.shape
    result = jax.ShapeDtypeStruct((frames, rows, cols, channels // 2), BF16)
    return pl.pallas_call(
        conv_kernel,
        out_shape=result,
        in_specs=whole(3 + len(around)),
        out_specs=pl.BlockSpec(memory_space=pl.ANY),
        scratch_shapes=[pltpu.VMEM(result.shape, BF16), pltpu.SemaphoreType.DMA((2, frames))],
        compiler_params=pltpu.CompilerParams(vmem_limit_bytes=VMEM_LIMIT),
        cost_estimate=pl.CostEstimate(
            flops=20 * hidden.size, bytes_accessed=4 * hidden.size, transcendentals=hidden.size // 2
        ),
        name="conv_gate",
    )(hidden, *around, weight, bias.reshape(-1, LANE))


ROW = ("row_far", "row_near")
GROUP = ("row_near", "col")


def across(value):
    n = lax.axis_size("row_far")
    return [
        lax.ppermute(value, "row_far", [(i, (i + step) % n) for i in range(n)])
        for step in range(1, n)
    ]


def exchange(value, step):
    n = lax.axis_size(GROUP)
    return lax.ppermute(value, GROUP, [(i, target(i, step, n)) for i in range(n)])


def frame_prefix(value):
    n, mine = lax.axis_size("frame"), lax.axis_index("frame")
    running = value
    doubling = n & (n - 1) == 0
    step = 1
    while step < n:
        pairs = [(i, i ^ step if doubling else (i + step) % n) for i in range(n)]
        got = lax.ppermute(value, "frame", pairs)
        running = running + jnp.where(mine & step != 0 if doubling else mine >= step, got, 0)
        value = value + got if doubling else value
        step = 2 * step if doubling else step + 1
    return running


def on_device(queries, keys, values, hidden, conv_weight, conv_bias):
    width = queries.shape[-1]
    tokens = queries.size // width
    pieces = lax.axis_size(GROUP)
    per = piece_rows(width, pieces)

    local = pl.pallas_call(
        functools.partial(state_kernel, width, pieces),
        out_shape=[jax.ShapeDtypeStruct((per // 8, 8, LANE), F32)] * pieces,
        in_specs=[pl.BlockSpec(memory_space=pltpu.HBM)] * 2,
        out_specs=whole(pieces),
        scratch_shapes=[
            pltpu.VMEM((tokens, width), BF16),
            pltpu.VMEM((tokens, width), BF16),
            pltpu.VMEM((pieces * per, LANE), F32),
            pltpu.SemaphoreType.DMA((2, 2)),
        ],
        compiler_params=pltpu.CompilerParams(vmem_limit_bytes=VMEM_MOST),
        cost_estimate=pl.CostEstimate(
            flops=2 * tokens * width * HD, bytes_accessed=6 * tokens * width, transcendentals=0
        ),
        name="local_state",
    )(keys.reshape(tokens, width), values.reshape(tokens, width))

    near = sum((exchange(local[step], step) for step in range(1, pieces)), local[0])
    near, (to_rows, to_cols) = lax.optimization_barrier((near, halo_sends(hidden)))
    block, by_cols, to_rows = lax.optimization_barrier(
        (sum(across(near), near), swap_columns(to_cols), to_rows)
    )

    prefix = frame_prefix(block)
    to_even, to_odd = with_corners(to_rows, by_cols)
    by_rows = swap_even_rows(to_even), swap_odd_rows(to_odd)
    quarters = [prefix, *(exchange(prefix, step) for step in range(1, pieces))]
    halos = (*by_rows, *by_cols)
    gated = convolve(hidden, halos, conv_weight, conv_bias)
    attended = pl.pallas_call(
        functools.partial(attend_kernel, width),
        out_shape=jax.ShapeDtypeStruct((tokens, width), BF16),
        in_specs=whole(1 + pieces),
        out_specs=pl.BlockSpec(memory_space=pl.ANY),
        scratch_shapes=[
            pltpu.VMEM((pieces * per, LANE), F32),
            pltpu.VMEM((tokens, width), BF16),
            pltpu.SemaphoreType.DMA((3,)),
        ],
        compiler_params=pltpu.CompilerParams(vmem_limit_bytes=VMEM_LIMIT),
        cost_estimate=pl.CostEstimate(
            flops=8 * tokens * width * HD, bytes_accessed=6 * tokens * width, transcendentals=0
        ),
        name="attend",
    )(queries.reshape(tokens, width), *quarters)
    return attended.reshape(queries.shape), gated


def solution(mesh):
    frame, row, col = (mesh.shape[name] for name in ("frame", "row", "col"))
    near = 2 if row % 2 == 0 else 1
    split = jax.sharding.Mesh(
        mesh.devices.reshape(frame, row // near, near, col), ("frame", *ROW, "col")
    )
    placed = P("frame", ROW, "col", None)
    return jax.shard_map(
        on_device,
        mesh=split,
        in_specs=(placed, placed, placed, placed, P(), P()),
        out_specs=(placed, placed),
        check_vma=False,
    )
```

```python
import functools

import jax
import jax.numpy as jnp
from jax import lax
from jax.experimental import pallas as pl
from jax.experimental.pallas import tpu as pltpu
from jax.sharding import PartitionSpec as P

HEADS = 70
HD = 32
EPS = 1e-06
LANE = 128
F32 = jnp.float32
BF16 = jnp.bfloat16
VMEM_LIMIT = 40 * 1024 * 1024
VMEM_MOST = 60 * 1024 * 1024


def whole(n):
    return [pl.BlockSpec(memory_space=pltpu.VMEM)] * n


def lane_tiles(width):
    return -(-width // LANE)


def piece_rows(width, pieces):
    return 8 * -(-lane_tiles(width) * (HD + 1) // (8 * pieces))


def target(place, step, n):
    return place ^ step if n & (n - 1) == 0 else (place + step) % n


def source(place, step, n):
    return place ^ step if n & (n - 1) == 0 else (place + n - step) % n


def piece(place, per):
    return pl.ds(pl.multiple_of(place * per, 8), per)


def same_head(shape):
    first = lax.broadcasted_iota(jnp.int32, shape, 0) // HD
    second = lax.broadcasted_iota(jnp.int32, shape, 1) // HD
    return first == second


def state_kernel(width, pieces, keys, values, *refs):
    *outs, k_ref, v_ref, held, sems = refs
    tokens = k_ref.shape[0]
    tiles = lane_tiles(width)
    half = tiles // 2
    loads = []
    for c, (lo, hi) in enumerate(((0, half * LANE), (half * LANE, width))):
        at = pl.ds(lo, hi - lo)
        for i, (array, ref) in enumerate(((keys, k_ref), (values, v_ref))):
            loads.append(pltpu.make_async_copy(array.at[:, at], ref.at[:, at], sems.at[c, i]))
            loads[-1].start()
    ones = jnp.ones((8, tokens), BF16)
    held[tiles * HD :, :] = jnp.zeros((held.shape[0] - tiles * HD, LANE), F32)
    for j in range(tiles):
        if j in (0, half):
            for copy in loads[2 * (j // half) : 2 * (j // half) + 2]:
                copy.wait()
        lo, hi = j * LANE, min(width, (j + 1) * LANE)
        n = hi - lo
        kpos = jnp.maximum(k_ref[:, lo:hi], 0)
        vals = v_ref[:, lo:hi]
        full = lax.dot_general(kpos, vals, (((0,), (0,)), ((), ())), preferred_element_type=F32)
        ksum = jnp.dot(ones, kpos, preferred_element_type=F32)
        head = lax.broadcasted_iota(jnp.int32, (HD, n), 1) // HD
        packed = jnp.zeros((HD, n), F32)
        for i in range(n // HD):
            packed = jnp.where(head == i, full[i * HD : (i + 1) * HD, :], packed)
        if n < LANE:
            held[j * HD : (j + 1) * HD, :] = jnp.zeros((HD, LANE), F32)
        held[j * HD : (j + 1) * HD, :n] = packed
        held[tiles * HD + j : tiles * HD + j + 1, :n] = ksum[:1]
    mine = lax.axis_index(GROUP)
    for step, out in enumerate(outs):
        rows = piece(target(mine, step, pieces), 8 * out.shape[0])
        out[...] = held[rows, :].reshape(out.shape)


def halves(x):
    high = x.astype(BF16)
    return high, (x - high.astype(F32)).astype(BF16)


def attend_kernel(width, q_ref, *refs):
    *quarters, out, p_ref, out_ref, sems = refs
    mine, pieces = lax.axis_index(GROUP), len(quarters)
    for step, quarter in enumerate(reversed(quarters)):
        rows = piece(source(mine, step, pieces), 8 * quarter.shape[0])
        p_ref[rows, :] = quarter[...].reshape(-1, LANE)
    tiles = lane_tiles(width)
    parts = sems.shape[0]
    firsts = [tiles * c // parts for c in range(parts + 1)]
    stores = []
    for j in range(tiles):
        lo, hi = j * LANE, min(width, (j + 1) * LANE)
        n = hi - lo
        qpos = jnp.maximum(q_ref[:, lo:hi], 0)
        same = same_head((n, n))
        part = p_ref[j * HD : (j + 1) * HD, :n]
        spread = jnp.where(same, jnp.concatenate([part] * (n // HD), axis=0), 0.0)
        zrow = p_ref[tiles * HD + j : tiles * HD + j + 1, :n]
        block = same.astype(F32).astype(BF16)
        numer = jnp.dot(
            jnp.concatenate([qpos, qpos], axis=1),
            jnp.concatenate(halves(spread), axis=0),
            preferred_element_type=F32,
        )
        denom = jnp.dot(
            jnp.concatenate(halves(qpos.astype(F32) * zrow), axis=1),
            jnp.concatenate([block, block], axis=0),
            preferred_element_type=F32,
        )
        out_ref[:, lo:hi] = (numer / (denom + EPS)).astype(BF16)
        if j + 1 in firsts:
            c = firsts.index(j + 1) - 1
            at = pl.ds(firsts[c] * LANE, hi - firsts[c] * LANE)
            stores.append(pltpu.make_async_copy(out_ref.at[:, at], out.at[:, at], sems.at[c]))
            stores[-1].start()
    for copy in stores:
        copy.wait()


def place(axis):
    return lax.axis_index(axis), lax.axis_size(axis)


def chosen(by_even, by_odd, mine, n):
    if n == 1:
        return jnp.zeros_like(by_even), jnp.zeros_like(by_even)
    if n == 2:
        return jnp.where(mine == 1, by_even, 0), jnp.where(mine == 0, by_even, 0)
    is_even = lax.rem(mine, 2) == 0
    before = jnp.where(is_even, by_odd, by_even)
    after = jnp.where(is_even, by_even, by_odd)
    return jnp.where(mine == 0, 0, before), jnp.where(mine == n - 1, 0, after)


def stored(frames, ends, held, out, sems, tile):
    stores = []
    for part, (lo, hi) in enumerate(zip(ends, ends[1:])):
        lax.fori_loop(lo, hi, tile, 0)
        at = pl.ds(lo * LANE, (hi - lo) * LANE)
        for f in range(frames):
            stores.append(
                pltpu.make_async_copy(
                    held.at[f, :, :, at], out.at[f, :, :, at], sems.at[part, f]
                )
            )
            stores[-1].start()
    for copy in stores:
        copy.wait()


def lane_tile(i):
    return pl.ds(pl.multiple_of(i * LANE, LANE), LANE)


def tap_rows(w, b):
    return [w[3 * a + b : 3 * a + b + 1] for a in range(3)]


def inside(tap, b, cols):
    spot = lax.broadcasted_iota(jnp.int32, (cols, LANE), 0)
    return tap if b == 1 else jnp.where(spot == (0 if b == 0 else cols - 1), 0.0, tap)


def moved(x, b, cols):
    return x if b == 1 else pltpu.roll(x, 1 if b == 0 else cols - 1, x.ndim - 2)


def inner_kernel(hidden, weight, bias, out, held, sems):
    frames, rows, cols, channels = hidden.shape
    steps, parts = channels // LANE, sems.shape[0]

    def tile(i, carry):
        at = lane_tile(i)
        w = weight[:, at]
        taps = [[inside(tap, b, cols)[None] for tap in tap_rows(w, b)] for b in range(3)]
        none = jnp.zeros((1, cols, LANE), F32)
        for f in range(frames):
            x = jnp.concatenate([none, hidden[f, :, :, at].astype(F32), none], axis=0)
            total = bias[pl.ds(i, 1), :][None]
            for b in range(3):
                y = moved(x, b, cols)
                total = total + sum(tap * y[a : a + rows] for a, tap in enumerate(taps[b]))
            held[f, :, :, at] = total
        return carry

    stored(frames, [steps * p // parts for p in range(parts + 1)], held, out, sems, tile)


def outer_kernel(inner, row_o, row_e, col_e, col_o, weight, out, held, sems):
    frames, rows, cols, channels = inner.shape
    half = channels // 2
    in_rows, (col, n_cols) = place(ROW), place("col")
    steps, parts = half // LANE, sems.shape[0]

    def conv(f, i):
        at = lane_tile(i)
        w = weight[:, at]
        spot = lax.broadcasted_iota(jnp.int32, (cols, LANE), 0)

        def part(ref, at=at):
            return ref[f, :, at].astype(F32)

        def corners(side):
            wide = -(-(channels // LANE) // cols)
            first = channels + (side * wide + lax.rem(i, wide)) * LANE
            lanes = pl.ds(pl.multiple_of(first, LANE), LANE)
            lines = chosen(part(row_e, lanes), part(row_o, lanes), *in_rows)
            return [pltpu.roll(x, lax.rem(cols - i // wide, cols), 0)[:1] for x in lines]

        def beside(taps, edge, top, end):
            z = jnp.concatenate([top, edge, end], axis=0)
            return sum(tap * z[a : a + rows] for a, tap in enumerate(taps))

        def line(x, a):
            return sum(
                inside(tap_rows(w, b)[a], b, cols) * moved(x, b, cols) for b in range(3)
            )

        up, down = chosen(part(row_e), part(row_o), *in_rows)
        top, end = line(up, 0), line(down, 2)
        if n_cols == 2:
            taps = [jnp.where(col == 0, r, l) for l, r in zip(tap_rows(w, 0), tap_rows(w, 2))]
            border = jnp.where(col == 0, cols - 1, 0)
            terms = [(border, beside(taps, part(col_e), *corners(0)))]
        else:
            edges = chosen(part(col_e), part(col_o), col, n_cols)
            terms = [
                (border, beside(tap_rows(w, b), edge, *corners(side)))
                for side, (border, b, edge) in enumerate(zip((0, cols - 1), (0, 2), edges))
                if n_cols > 1
            ]
        total = []
        for r in range(rows):
            here = inner[f, r, :, at]
            for border, term in terms:
                here = here + jnp.where(spot == border, term[r : r + 1], 0.0)
            here = here + top if r == 0 else here
            total.append(here + end if r == rows - 1 else here)
        return total

    def tile(i, carry):
        for f in range(frames):
            for r, (value, gate) in enumerate(zip(conv(f, i), conv(f, i + steps))):
                held[f, r, :, lane_tile(i)] = (
                    0.5 * value * gate * (1.0 + jnp.tanh(0.5 * gate))
                ).astype(BF16)
        return carry

    stored(frames, [steps * p // parts for p in range(parts + 1)], held, out, sems, tile)


def swaps(n):
    even = [min(i ^ 1, n - 1) for i in range(n)]
    odd = [min(max(((i - 1) ^ 1) + 1, 0), n - 1) for i in range(n)]
    return [list(enumerate(to)) for to in ((even, odd) if n > 2 else (even,))]


def sends(first, last, axis):
    is_even = lax.rem(lax.axis_index(axis), 2) == 0
    return jnp.where(is_even, last, first), jnp.where(is_even, first, last)


def halo_sends(hidden):
    rows, cols = hidden.shape[1:3]
    to_rows = sends(hidden[:, 0], hidden[:, rows - 1], ROW)
    return to_rows, sends(hidden[:, :, 0], hidden[:, :, cols - 1], "col")


def with_corners(to_rows, by_cols):
    frames, cols, channels = to_rows[0].shape
    n_cols = lax.axis_size("col")
    if n_cols == 1:
        return to_rows
    sides = by_cols[:1] if n_cols == 2 else chosen(*by_cols, *place("col"))
    wide = -(-channels // (cols * LANE)) * LANE
    packed = []
    for side in sides:
        corners = sends(side[:, 0], side[:, side.shape[1] - 1], ROW)
        spare = ((0, 0), (0, cols * wide - channels))
        packed.append([jnp.pad(x, spare).reshape(frames, cols, wide) for x in corners])
    return [jnp.concatenate(parts, axis=2) for parts in zip(to_rows, *packed)]


def both(results):
    return [results[0], results[-1]]


def swap_even_rows(to_even):
    return lax.ppermute(to_even, ROW, swaps(lax.axis_size(ROW))[0])


def swap_odd_rows(to_odd):
    pairs = swaps(lax.axis_size(ROW))[1:]
    return lax.ppermute(to_odd, ROW, pairs[0]) if pairs else to_odd


def swap_columns(to_cols):
    pairs = swaps(lax.axis_size("col"))
    return both([lax.ppermute(x, "col", p) for x, p in zip(to_cols, pairs)])


def convolve(kernel, name, result, *arrays):
    return pl.pallas_call(
        kernel,
        out_shape=result,
        in_specs=whole(len(arrays)),
        out_specs=pl.BlockSpec(memory_space=pl.ANY),
        scratch_shapes=[
            pltpu.VMEM(result.shape, result.dtype),
            pltpu.SemaphoreType.DMA((2, result.shape[0])),
        ],
        compiler_params=pltpu.CompilerParams(vmem_limit_bytes=VMEM_LIMIT),
        cost_estimate=pl.CostEstimate(
            flops=20 * result.size, bytes_accessed=6 * result.size, transcendentals=0
        ),
        name=name,
    )(*arrays)


ROW = ("row_far", "row_near")
GROUP = ("row_near", "col")


def across(value):
    n = lax.axis_size("row_far")
    return [
        lax.ppermute(value, "row_far", [(i, (i + step) % n) for i in range(n)])
        for step in range(1, n)
    ]


def exchange(value, step):
    n = lax.axis_size(GROUP)
    return lax.ppermute(value, GROUP, [(i, target(i, step, n)) for i in range(n)])


def frame_prefix(value):
    n, mine = lax.axis_size("frame"), lax.axis_index("frame")
    running = value
    doubling = n & (n - 1) == 0
    step = 1
    while step < n:
        pairs = [(i, i ^ step if doubling else (i + step) % n) for i in range(n)]
        got = lax.ppermute(value, "frame", pairs)
        running = running + jnp.where(mine & step != 0 if doubling else mine >= step, got, 0)
        value = value + got if doubling else value
        step = 2 * step if doubling else step + 1
    return running


def on_device(queries, keys, values, hidden, conv_weight, conv_bias):
    width = queries.shape[-1]
    tokens = queries.size // width
    pieces = lax.axis_size(GROUP)
    per = piece_rows(width, pieces)

    local = pl.pallas_call(
        functools.partial(state_kernel, width, pieces),
        out_shape=[jax.ShapeDtypeStruct((per // 8, 8, LANE), F32)] * pieces,
        in_specs=[pl.BlockSpec(memory_space=pltpu.HBM)] * 2,
        out_specs=whole(pieces),
        scratch_shapes=[
            pltpu.VMEM((tokens, width), BF16),
            pltpu.VMEM((tokens, width), BF16),
            pltpu.VMEM((pieces * per, LANE), F32),
            pltpu.SemaphoreType.DMA((2, 2)),
        ],
        compiler_params=pltpu.CompilerParams(vmem_limit_bytes=VMEM_MOST),
        cost_estimate=pl.CostEstimate(
            flops=2 * tokens * width * HD, bytes_accessed=6 * tokens * width, transcendentals=0
        ),
        name="local_state",
    )(keys.reshape(tokens, width), values.reshape(tokens, width))

    near = sum((exchange(local[step], step) for step in range(1, pieces)), local[0])
    near, (to_rows, to_cols), bias = lax.optimization_barrier(
        (near, halo_sends(hidden), conv_bias)
    )
    summed = jax.ShapeDtypeStruct(hidden.shape, F32)
    inner = convolve(
        inner_kernel, "conv_inner", summed, hidden, conv_weight, bias.reshape(-1, LANE)
    )
    block, by_cols, to_rows, inner = lax.optimization_barrier(
        (sum(across(near), near), swap_columns(to_cols), to_rows, inner)
    )

    to_even, to_odd = with_corners(to_rows, by_cols)
    prefix = frame_prefix(block)
    by_rows = swap_even_rows(to_even), swap_odd_rows(to_odd)
    others = [exchange(prefix, step) for step in range(pieces - 1, 0, -1)]
    halos = (*by_rows[::-1], *by_cols)
    result = jax.ShapeDtypeStruct((*hidden.shape[:3], hidden.shape[3] // 2), BF16)
    gated = convolve(outer_kernel, "conv_gate", result, inner, *halos, conv_weight)
    others, gated = lax.optimization_barrier((others, gated))
    attended = pl.pallas_call(
        functools.partial(attend_kernel, width),
        out_shape=jax.ShapeDtypeStruct((tokens, width), BF16),
        in_specs=whole(1 + pieces),
        out_specs=pl.BlockSpec(memory_space=pl.ANY),
        scratch_shapes=[
            pltpu.VMEM((pieces * per, LANE), F32),
            pltpu.VMEM((tokens, width), BF16),
            pltpu.SemaphoreType.DMA((3,)),
        ],
        compiler_params=pltpu.CompilerParams(vmem_limit_bytes=VMEM_LIMIT),
        cost_estimate=pl.CostEstimate(
            flops=8 * tokens * width * HD, bytes_accessed=6 * tokens * width, transcendentals=0
        ),
        name="attend",
    )(queries.reshape(tokens, width), *others, prefix)
    return attended.reshape(queries.shape), gated


def solution(mesh):
    frame, row, col = (mesh.shape[name] for name in ("frame", "row", "col"))
    near = 2 if row % 2 == 0 else 1
    split = jax.sharding.Mesh(
        mesh.devices.reshape(frame, row // near, near, col), ("frame", *ROW, "col")
    )
    placed = P("frame", ROW, "col", None)
    return jax.shard_map(
        on_device,
        mesh=split,
        in_specs=(placed, placed, placed, placed, P(), P()),
        out_specs=(placed, placed),
        check_vma=False,
    )
```

```python
import functools

import jax
import jax.numpy as jnp
from jax import lax
from jax.experimental import pallas as pl
from jax.experimental.pallas import tpu as pltpu
from jax.sharding import PartitionSpec as P

HEADS = 70
HD = 32
EPS = 1e-06
LANE = 128
F32 = jnp.float32
BF16 = jnp.bfloat16
VMEM_LIMIT = 40 * 1024 * 1024
VMEM_MOST = 60 * 1024 * 1024


def whole(n):
    return [pl.BlockSpec(memory_space=pltpu.VMEM)] * n


def lane_tiles(width):
    return -(-width // LANE)


def piece_rows(width, pieces):
    return 8 * -(-lane_tiles(width) * (HD + 1) // (8 * pieces))


def target(place, step, n):
    return place ^ step if n & (n - 1) == 0 else (place + step) % n


def source(place, step, n):
    return place ^ step if n & (n - 1) == 0 else (place + n - step) % n


def piece(place, per):
    return pl.ds(pl.multiple_of(place * per, 8), per)


def same_head(shape):
    first = lax.broadcasted_iota(jnp.int32, shape, 0) // HD
    second = lax.broadcasted_iota(jnp.int32, shape, 1) // HD
    return first == second


def state_kernel(width, pieces, keys, values, *refs):
    *outs, k_ref, v_ref, held, sems, store_sems = refs
    tokens = k_ref.shape[0]
    tiles = lane_tiles(width)
    half = tiles // 2
    loads = []
    for c, (lo, hi) in enumerate(((0, half * LANE), (half * LANE, width))):
        at = pl.ds(lo, hi - lo)
        for i, (array, ref) in enumerate(((keys, k_ref), (values, v_ref))):
            loads.append(pltpu.make_async_copy(array.at[:, at], ref.at[:, at], sems.at[c, i]))
            loads[-1].start()
    mine = lax.axis_index(GROUP)
    per = outs[0].shape[0]

    def store(k, step):
        return pltpu.make_async_copy(
            held.at[pl.ds(k * per, per)], outs[step], store_sems.at[step]
        )

    ones = jnp.ones((8, tokens), BF16)
    groups = HD // 8
    held[tiles * groups :] = jnp.zeros((held.shape[0] - tiles * groups, 8, LANE), F32)
    sent = 0
    for j in range(tiles):
        if j in (0, half):
            for copy in loads[2 * (j // half) : 2 * (j // half) + 2]:
                copy.wait()
        lo, hi = j * LANE, min(width, (j + 1) * LANE)
        n = hi - lo
        kpos = jnp.maximum(k_ref[:, lo:hi], 0)
        vals = v_ref[:, lo:hi]
        full = lax.dot_general(kpos, vals, (((0,), (0,)), ((), ())), preferred_element_type=F32)
        ksum = jnp.dot(ones, kpos, preferred_element_type=F32)
        head = lax.broadcasted_iota(jnp.int32, (HD, n), 1) // HD
        packed = jnp.zeros((HD, n), F32)
        for i in range(n // HD):
            packed = jnp.where(head == i, full[i * HD : (i + 1) * HD, :], packed)
        if n < LANE:
            held[j * groups : (j + 1) * groups] = jnp.zeros((groups, 8, LANE), F32)
        held[j * groups : (j + 1) * groups, :, :n] = packed.reshape(groups, 8, n)
        held[tiles * groups + j // 8, j % 8 : j % 8 + 1, :n] = ksum[:1]
        done = pieces if j == tiles - 1 else (j + 1) * groups // per
        for k in range(sent, done):
            for step in range(pieces):
                pl.when(target(mine, step, pieces) == k)(store(k, step).start)
        sent = done
    for step in range(pieces):
        store(0, step).wait()


def halves(x):
    high = x.astype(BF16)
    return high, (x - high.astype(F32)).astype(BF16)


def attend_kernel(width, q_ref, *refs):
    *quarters, out, p_ref, out_ref, sems = refs
    mine, pieces = lax.axis_index(GROUP), len(quarters)
    for step, quarter in enumerate(reversed(quarters)):
        rows = piece(source(mine, step, pieces), 8 * quarter.shape[0])
        p_ref[rows, :] = quarter[...].reshape(-1, LANE)
    tiles = lane_tiles(width)
    parts = sems.shape[0]
    firsts = [tiles * c // parts for c in range(parts + 1)]
    stores = []
    for j in range(tiles):
        lo, hi = j * LANE, min(width, (j + 1) * LANE)
        n = hi - lo
        qpos = jnp.maximum(q_ref[:, lo:hi], 0)
        same = same_head((n, n))
        part = p_ref[j * HD : (j + 1) * HD, :n]
        spread = jnp.where(same, jnp.concatenate([part] * (n // HD), axis=0), 0.0)
        zrow = p_ref[tiles * HD + j : tiles * HD + j + 1, :n]
        block = same.astype(F32).astype(BF16)
        numer = jnp.dot(
            jnp.concatenate([qpos, qpos], axis=1),
            jnp.concatenate(halves(spread), axis=0),
            preferred_element_type=F32,
        )
        denom = jnp.dot(
            jnp.concatenate(halves(qpos.astype(F32) * zrow), axis=1),
            jnp.concatenate([block, block], axis=0),
            preferred_element_type=F32,
        )
        out_ref[:, lo:hi] = (numer / (denom + EPS)).astype(BF16)
        if j + 1 in firsts:
            c = firsts.index(j + 1) - 1
            at = pl.ds(firsts[c] * LANE, hi - firsts[c] * LANE)
            stores.append(pltpu.make_async_copy(out_ref.at[:, at], out.at[:, at], sems.at[c]))
            stores[-1].start()
    for copy in stores:
        copy.wait()


def place(axis):
    return lax.axis_index(axis), lax.axis_size(axis)


def chosen(by_even, by_odd, mine, n):
    if n == 1:
        return jnp.zeros_like(by_even), jnp.zeros_like(by_even)
    if n == 2:
        return jnp.where(mine == 1, by_even, 0), jnp.where(mine == 0, by_even, 0)
    is_even = lax.rem(mine, 2) == 0
    before = jnp.where(is_even, by_odd, by_even)
    after = jnp.where(is_even, by_even, by_odd)
    return jnp.where(mine == 0, 0, before), jnp.where(mine == n - 1, 0, after)


def stored(frames, ends, held, out, sems, tile):
    stores = []
    for part, (lo, hi) in enumerate(zip(ends, ends[1:])):
        lax.fori_loop(lo, hi, tile, 0)
        at = pl.ds(lo * LANE, (hi - lo) * LANE)
        for f in range(frames):
            stores.append(
                pltpu.make_async_copy(
                    held.at[f, :, :, at], out.at[f, :, :, at], sems.at[part, f]
                )
            )
            stores[-1].start()
    for copy in stores:
        copy.wait()


def lane_tile(i):
    return pl.ds(pl.multiple_of(i * LANE, LANE), LANE)


def tap_rows(w, b):
    return [w[3 * a + b : 3 * a + b + 1] for a in range(3)]


def inside(tap, b, cols):
    spot = lax.broadcasted_iota(jnp.int32, (cols, LANE), 0)
    return tap if b == 1 else jnp.where(spot == (0 if b == 0 else cols - 1), 0.0, tap)


def moved(x, b, cols):
    return x if b == 1 else pltpu.roll(x, 1 if b == 0 else cols - 1, x.ndim - 2)


def inner_kernel(hidden, weight, bias, out, held, sems):
    frames, rows, cols, channels = hidden.shape
    steps, parts = channels // LANE, sems.shape[0]

    def tile(i, carry):
        at = lane_tile(i)
        w = weight[:, at]
        taps = [[inside(tap, b, cols)[None] for tap in tap_rows(w, b)] for b in range(3)]
        none = jnp.zeros((1, cols, LANE), F32)
        for f in range(frames):
            x = jnp.concatenate([none, hidden[f, :, :, at].astype(F32), none], axis=0)
            total = bias[pl.ds(i, 1), :][None]
            for b in range(3):
                y = moved(x, b, cols)
                total = total + sum(tap * y[a : a + rows] for a, tap in enumerate(taps[b]))
            held[f, :, :, at] = total
        return carry

    stored(frames, [steps * p // parts for p in range(parts + 1)], held, out, sems, tile)


def outer_kernel(inner, row_o, row_e, col_e, col_o, weight, out, held, sems):
    frames, rows, cols, channels = inner.shape
    half = channels // 2
    in_rows, (col, n_cols) = place(ROW), place("col")
    steps, parts = half // LANE, sems.shape[0]

    def conv(f, i):
        at = lane_tile(i)
        w = weight[:, at]
        spot = lax.broadcasted_iota(jnp.int32, (cols, LANE), 0)

        def part(ref, at=at):
            return ref[f, :, at].astype(F32)

        def corners(side):
            wide = -(-(channels // LANE) // cols)
            first = channels + (side * wide + lax.rem(i, wide)) * LANE
            lanes = pl.ds(pl.multiple_of(first, LANE), LANE)
            lines = chosen(part(row_e, lanes), part(row_o, lanes), *in_rows)
            return [pltpu.roll(x, lax.rem(cols - i // wide, cols), 0)[:1] for x in lines]

        def beside(taps, edge, top, end):
            z = jnp.concatenate([top, edge, end], axis=0)
            return sum(tap * z[a : a + rows] for a, tap in enumerate(taps))

        def line(x, a):
            return sum(
                inside(tap_rows(w, b)[a], b, cols) * moved(x, b, cols) for b in range(3)
            )

        up, down = chosen(part(row_e), part(row_o), *in_rows)
        top, end = line(up, 0), line(down, 2)
        if n_cols == 2:
            taps = [jnp.where(col == 0, r, l) for l, r in zip(tap_rows(w, 0), tap_rows(w, 2))]
            border = jnp.where(col == 0, cols - 1, 0)
            terms = [(border, beside(taps, part(col_e), *corners(0)))]
        else:
            edges = chosen(part(col_e), part(col_o), col, n_cols)
            terms = [
                (border, beside(tap_rows(w, b), edge, *corners(side)))
                for side, (border, b, edge) in enumerate(zip((0, cols - 1), (0, 2), edges))
                if n_cols > 1
            ]
        total = []
        for r in range(rows):
            here = inner[f, r, :, at]
            for border, term in terms:
                here = here + jnp.where(spot == border, term[r : r + 1], 0.0)
            here = here + top if r == 0 else here
            total.append(here + end if r == rows - 1 else here)
        return total

    def tile(i, carry):
        for f in range(frames):
            for r, (value, gate) in enumerate(zip(conv(f, i), conv(f, i + steps))):
                held[f, r, :, lane_tile(i)] = (
                    0.5 * value * gate * (1.0 + jnp.tanh(0.5 * gate))
                ).astype(BF16)
        return carry

    stored(frames, [steps * p // parts for p in range(parts + 1)], held, out, sems, tile)


def swaps(n):
    even = [min(i ^ 1, n - 1) for i in range(n)]
    odd = [min(max(((i - 1) ^ 1) + 1, 0), n - 1) for i in range(n)]
    return [list(enumerate(to)) for to in ((even, odd) if n > 2 else (even,))]


def sends(first, last, axis):
    is_even = lax.rem(lax.axis_index(axis), 2) == 0
    return jnp.where(is_even, last, first), jnp.where(is_even, first, last)


def halo_sends(hidden):
    rows, cols = hidden.shape[1:3]
    to_rows = sends(hidden[:, 0], hidden[:, rows - 1], ROW)
    return to_rows, sends(hidden[:, :, 0], hidden[:, :, cols - 1], "col")


def with_corners(to_rows, by_cols):
    frames, cols, channels = to_rows[0].shape
    n_cols = lax.axis_size("col")
    if n_cols == 1:
        return to_rows
    sides = by_cols[:1] if n_cols == 2 else chosen(*by_cols, *place("col"))
    wide = -(-channels // (cols * LANE)) * LANE
    packed = []
    for side in sides:
        corners = sends(side[:, 0], side[:, side.shape[1] - 1], ROW)
        spare = ((0, 0), (0, cols * wide - channels))
        packed.append([jnp.pad(x, spare).reshape(frames, cols, wide) for x in corners])
    return [jnp.concatenate(parts, axis=2) for parts in zip(to_rows, *packed)]


def both(results):
    return [results[0], results[-1]]


def swap_even_rows(to_even):
    return lax.ppermute(to_even, ROW, swaps(lax.axis_size(ROW))[0])


def swap_odd_rows(to_odd):
    pairs = swaps(lax.axis_size(ROW))[1:]
    return lax.ppermute(to_odd, ROW, pairs[0]) if pairs else to_odd


def swap_columns(to_cols):
    pairs = swaps(lax.axis_size("col"))
    return both([lax.ppermute(x, "col", p) for x, p in zip(to_cols, pairs)])


def convolve(kernel, name, result, *arrays):
    return pl.pallas_call(
        kernel,
        out_shape=result,
        in_specs=whole(len(arrays)),
        out_specs=pl.BlockSpec(memory_space=pl.ANY),
        scratch_shapes=[
            pltpu.VMEM(result.shape, result.dtype),
            pltpu.SemaphoreType.DMA((2, result.shape[0])),
        ],
        compiler_params=pltpu.CompilerParams(vmem_limit_bytes=VMEM_LIMIT),
        cost_estimate=pl.CostEstimate(
            flops=20 * result.size, bytes_accessed=6 * result.size, transcendentals=0
        ),
        name=name,
    )(*arrays)


ROW = ("row_far", "row_near")
GROUP = ("row_near", "col")


def across(value):
    n = lax.axis_size("row_far")
    return [
        lax.ppermute(value, "row_far", [(i, (i + step) % n) for i in range(n)])
        for step in range(1, n)
    ]


def exchange(value, step):
    n = lax.axis_size(GROUP)
    return lax.ppermute(value, GROUP, [(i, target(i, step, n)) for i in range(n)])


def frame_prefix(value):
    n, mine = lax.axis_size("frame"), lax.axis_index("frame")
    running = value
    doubling = n & (n - 1) == 0
    step = 1
    while step < n:
        pairs = [(i, i ^ step if doubling else (i + step) % n) for i in range(n)]
        got = lax.ppermute(value, "frame", pairs)
        running = running + jnp.where(mine & step != 0 if doubling else mine >= step, got, 0)
        value = value + got if doubling else value
        step = 2 * step if doubling else step + 1
    return running


def on_device(queries, keys, values, hidden, conv_weight, conv_bias):
    width = queries.shape[-1]
    tokens = queries.size // width
    pieces = lax.axis_size(GROUP)
    per = piece_rows(width, pieces)

    local = pl.pallas_call(
        functools.partial(state_kernel, width, pieces),
        out_shape=[jax.ShapeDtypeStruct((per // 8, 8, LANE), F32)] * pieces,
        in_specs=[pl.BlockSpec(memory_space=pltpu.HBM)] * 2,
        out_specs=[pl.BlockSpec(memory_space=pl.ANY)] * pieces,
        scratch_shapes=[
            pltpu.VMEM((tokens, width), BF16),
            pltpu.VMEM((tokens, width), BF16),
            pltpu.VMEM((pieces * per // 8, 8, LANE), F32),
            pltpu.SemaphoreType.DMA((2, 2)),
            pltpu.SemaphoreType.DMA((pieces,)),
        ],
        compiler_params=pltpu.CompilerParams(vmem_limit_bytes=VMEM_MOST),
        cost_estimate=pl.CostEstimate(
            flops=2 * tokens * width * HD, bytes_accessed=6 * tokens * width, transcendentals=0
        ),
        name="local_state",
    )(keys.reshape(tokens, width), values.reshape(tokens, width))

    near = sum((exchange(local[step], step) for step in range(1, pieces)), local[0])
    near, (to_rows, to_cols), bias = lax.optimization_barrier(
        (near, halo_sends(hidden), conv_bias)
    )
    summed = jax.ShapeDtypeStruct(hidden.shape, F32)
    inner = convolve(
        inner_kernel, "conv_inner", summed, hidden, conv_weight, bias.reshape(-1, LANE)
    )
    block, by_cols, to_rows, inner = lax.optimization_barrier(
        (sum(across(near), near), swap_columns(to_cols), to_rows, inner)
    )

    to_even, to_odd = with_corners(to_rows, by_cols)
    prefix = frame_prefix(block)
    by_rows = swap_even_rows(to_even), swap_odd_rows(to_odd)
    others = [exchange(prefix, step) for step in range(pieces - 1, 0, -1)]
    halos = (*by_rows[::-1], *by_cols)
    result = jax.ShapeDtypeStruct((*hidden.shape[:3], hidden.shape[3] // 2), BF16)
    gated = convolve(outer_kernel, "conv_gate", result, inner, *halos, conv_weight)
    others, gated = lax.optimization_barrier((others, gated))
    attended = pl.pallas_call(
        functools.partial(attend_kernel, width),
        out_shape=jax.ShapeDtypeStruct((tokens, width), BF16),
        in_specs=whole(1 + pieces),
        out_specs=pl.BlockSpec(memory_space=pl.ANY),
        scratch_shapes=[
            pltpu.VMEM((pieces * per, LANE), F32),
            pltpu.VMEM((tokens, width), BF16),
            pltpu.SemaphoreType.DMA((3,)),
        ],
        compiler_params=pltpu.CompilerParams(vmem_limit_bytes=VMEM_LIMIT),
        cost_estimate=pl.CostEstimate(
            flops=8 * tokens * width * HD, bytes_accessed=6 * tokens * width, transcendentals=0
        ),
        name="attend",
    )(queries.reshape(tokens, width), *others, prefix)
    return attended.reshape(queries.shape), gated


def solution(mesh):
    frame, row, col = (mesh.shape[name] for name in ("frame", "row", "col"))
    near = 2 if row % 2 == 0 else 1
    split = jax.sharding.Mesh(
        mesh.devices.reshape(frame, row // near, near, col), ("frame", *ROW, "col")
    )
    placed = P("frame", ROW, "col", None)
    return jax.shard_map(
        on_device,
        mesh=split,
        in_specs=(placed, placed, placed, placed, P(), P()),
        out_specs=(placed, placed),
        check_vma=False,
    )
```

```python
import functools

import jax
import jax.numpy as jnp
from jax import lax
from jax.experimental import pallas as pl
from jax.experimental.pallas import tpu as pltpu
from jax.sharding import PartitionSpec as P

HEADS = 70
HD = 32
EPS = 1e-06
LANE = 128
F32 = jnp.float32
BF16 = jnp.bfloat16
VMEM_LIMIT = 40 * 1024 * 1024
VMEM_MOST = 60 * 1024 * 1024


def whole(n):
    return [pl.BlockSpec(memory_space=pltpu.VMEM)] * n


def lane_tiles(width):
    return -(-width // LANE)


def piece_rows(width, pieces):
    return 8 * -(-lane_tiles(width) * (HD + 1) // (8 * pieces))


def target(place, step, n):
    return place ^ step if n & (n - 1) == 0 else (place + step) % n


def source(place, step, n):
    return place ^ step if n & (n - 1) == 0 else (place + n - step) % n


def piece(place, per):
    return pl.ds(pl.multiple_of(place * per, 8), per)


def same_head(shape):
    first = lax.broadcasted_iota(jnp.int32, shape, 0) // HD
    second = lax.broadcasted_iota(jnp.int32, shape, 1) // HD
    return first == second


def state_kernel(width, pieces, keys, values, *refs):
    *outs, k_ref, v_ref, held, sems = refs
    tokens = k_ref.shape[0]
    tiles = lane_tiles(width)
    half = tiles // 2
    loads = []
    for c, (lo, hi) in enumerate(((0, half * LANE), (half * LANE, width))):
        at = pl.ds(lo, hi - lo)
        for i, (array, ref) in enumerate(((keys, k_ref), (values, v_ref))):
            loads.append(pltpu.make_async_copy(array.at[:, at], ref.at[:, at], sems.at[c, i]))
            loads[-1].start()
    ones = jnp.ones((8, tokens), BF16)
    held[tiles * HD :, :] = jnp.zeros((held.shape[0] - tiles * HD, LANE), F32)
    for j in range(tiles):
        if j in (0, half):
            for copy in loads[2 * (j // half) : 2 * (j // half) + 2]:
                copy.wait()
        lo, hi = j * LANE, min(width, (j + 1) * LANE)
        n = hi - lo
        kpos = jnp.maximum(k_ref[:, lo:hi], 0)
        vals = v_ref[:, lo:hi]
        full = lax.dot_general(kpos, vals, (((0,), (0,)), ((), ())), preferred_element_type=F32)
        ksum = jnp.dot(ones, kpos, preferred_element_type=F32)
        head = lax.broadcasted_iota(jnp.int32, (HD, n), 1) // HD
        packed = jnp.zeros((HD, n), F32)
        for i in range(n // HD):
            packed = jnp.where(head == i, full[i * HD : (i + 1) * HD, :], packed)
        if n < LANE:
            held[j * HD : (j + 1) * HD, :] = jnp.zeros((HD, LANE), F32)
        held[j * HD : (j + 1) * HD, :n] = packed
        held[tiles * HD + j : tiles * HD + j + 1, :n] = ksum[:1]
    mine = lax.axis_index(GROUP)
    for step, out in enumerate(outs):
        rows = piece(target(mine, step, pieces), 8 * out.shape[0])
        out[...] = held[rows, :].reshape(out.shape)


def halves(x):
    high = x.astype(BF16)
    return high, (x - high.astype(F32)).astype(BF16)


def attend_kernel(width, q_ref, *refs):
    *quarters, out, p_ref, out_ref, sems = refs
    mine, pieces = lax.axis_index(GROUP), len(quarters)
    for step, quarter in enumerate(reversed(quarters)):
        rows = piece(source(mine, step, pieces), 8 * quarter.shape[0])
        p_ref[rows, :] = quarter[...].reshape(-1, LANE)
    tiles = lane_tiles(width)
    parts = sems.shape[0]
    firsts = [tiles * c // parts for c in range(parts + 1)]
    stores = []
    for j in range(tiles):
        lo, hi = j * LANE, min(width, (j + 1) * LANE)
        n = hi - lo
        qpos = jnp.maximum(q_ref[:, lo:hi], 0)
        same = same_head((n, n))
        part = p_ref[j * HD : (j + 1) * HD, :n]
        spread = jnp.where(same, jnp.concatenate([part] * (n // HD), axis=0), 0.0)
        zrow = p_ref[tiles * HD + j : tiles * HD + j + 1, :n]
        block = same.astype(F32).astype(BF16)
        numer = jnp.dot(
            jnp.concatenate([qpos, qpos], axis=1),
            jnp.concatenate(halves(spread), axis=0),
            preferred_element_type=F32,
        )
        denom = jnp.dot(
            jnp.concatenate(halves(qpos.astype(F32) * zrow), axis=1),
            jnp.concatenate([block, block], axis=0),
            preferred_element_type=F32,
        )
        out_ref[:, lo:hi] = (numer / (denom + EPS)).astype(BF16)
        if j + 1 in firsts:
            c = firsts.index(j + 1) - 1
            at = pl.ds(firsts[c] * LANE, hi - firsts[c] * LANE)
            stores.append(pltpu.make_async_copy(out_ref.at[:, at], out.at[:, at], sems.at[c]))
            stores[-1].start()
    for copy in stores:
        copy.wait()


def place(axis):
    return lax.axis_index(axis), lax.axis_size(axis)


def chosen(by_even, by_odd, mine, n):
    if n == 1:
        return jnp.zeros_like(by_even), jnp.zeros_like(by_even)
    if n == 2:
        return jnp.where(mine == 1, by_even, 0), jnp.where(mine == 0, by_even, 0)
    is_even = lax.rem(mine, 2) == 0
    before = jnp.where(is_even, by_odd, by_even)
    after = jnp.where(is_even, by_even, by_odd)
    return jnp.where(mine == 0, 0, before), jnp.where(mine == n - 1, 0, after)


def stored(frames, ends, held, out, sems, tile):
    stores = []
    for part, (lo, hi) in enumerate(zip(ends, ends[1:])):
        lax.fori_loop(lo, hi, tile, 0)
        at = pl.ds(lo * LANE, (hi - lo) * LANE)
        for f in range(frames):
            stores.append(
                pltpu.make_async_copy(
                    held.at[f, :, :, at], out.at[f, :, :, at], sems.at[part, f]
                )
            )
            stores[-1].start()
    for copy in stores:
        copy.wait()


def lane_tile(i):
    return pl.ds(pl.multiple_of(i * LANE, LANE), LANE)


def tap_rows(w, b):
    return [w[3 * a + b : 3 * a + b + 1] for a in range(3)]


def inside(tap, b, cols):
    spot = lax.broadcasted_iota(jnp.int32, (cols, LANE), 0)
    return tap if b == 1 else jnp.where(spot == (0 if b == 0 else cols - 1), 0.0, tap)


def moved(x, b, cols):
    return x if b == 1 else pltpu.roll(x, 1 if b == 0 else cols - 1, x.ndim - 2)


def inner_kernel(hidden, weight, bias, out, held, sems):
    frames, rows, cols, channels = hidden.shape
    steps, parts = channels // LANE, sems.shape[0]

    def tile(i, carry):
        at = lane_tile(i)
        w = weight[:, at]
        taps = [[inside(tap, b, cols)[None] for tap in tap_rows(w, b)] for b in range(3)]
        none = jnp.zeros((1, cols, LANE), F32)
        for f in range(frames):
            x = jnp.concatenate([none, hidden[f, :, :, at].astype(F32), none], axis=0)
            total = bias[pl.ds(i, 1), :][None]
            for b in range(3):
                y = moved(x, b, cols)
                total = total + sum(tap * y[a : a + rows] for a, tap in enumerate(taps[b]))
            held[f, :, :, at] = total
        return carry

    stored(frames, [steps * p // parts for p in range(parts + 1)], held, out, sems, tile)


def outer_kernel(inner, row_o, row_e, col_e, col_o, weight, out, held, sems):
    frames, rows, cols, channels = inner.shape
    half = channels // 2
    in_rows, (col, n_cols) = place(ROW), place("col")
    steps, parts = half // LANE, sems.shape[0]

    def conv(f, i):
        at = lane_tile(i)
        w = weight[:, at]
        spot = lax.broadcasted_iota(jnp.int32, (cols, LANE), 0)

        def part(ref, at=at):
            return ref[f, :, at].astype(F32)

        def corners(side):
            wide = -(-(channels // LANE) // cols)
            first = channels + (side * wide + lax.rem(i, wide)) * LANE
            lanes = pl.ds(pl.multiple_of(first, LANE), LANE)
            lines = chosen(part(row_e, lanes), part(row_o, lanes), *in_rows)
            return [pltpu.roll(x, lax.rem(cols - i // wide, cols), 0)[:1] for x in lines]

        def beside(taps, edge, top, end):
            z = jnp.concatenate([top, edge, end], axis=0)
            return sum(tap * z[a : a + rows] for a, tap in enumerate(taps))

        def line(x, a):
            return sum(
                inside(tap_rows(w, b)[a], b, cols) * moved(x, b, cols) for b in range(3)
            )

        up, down = chosen(part(row_e), part(row_o), *in_rows)
        top, end = line(up, 0), line(down, 2)
        if n_cols == 2:
            taps = [jnp.where(col == 0, r, l) for l, r in zip(tap_rows(w, 0), tap_rows(w, 2))]
            border = jnp.where(col == 0, cols - 1, 0)
            terms = [(border, beside(taps, part(col_e), *corners(0)))]
        else:
            edges = chosen(part(col_e), part(col_o), col, n_cols)
            terms = [
                (border, beside(tap_rows(w, b), edge, *corners(side)))
                for side, (border, b, edge) in enumerate(zip((0, cols - 1), (0, 2), edges))
                if n_cols > 1
            ]
        total = []
        for r in range(rows):
            here = inner[f, r, :, at]
            for border, term in terms:
                here = here + jnp.where(spot == border, term[r : r + 1], 0.0)
            here = here + top if r == 0 else here
            total.append(here + end if r == rows - 1 else here)
        return total

    def tile(i, carry):
        for f in range(frames):
            for r, (value, gate) in enumerate(zip(conv(f, i), conv(f, i + steps))):
                held[f, r, :, lane_tile(i)] = (
                    0.5 * value * gate * (1.0 + jnp.tanh(0.5 * gate))
                ).astype(BF16)
        return carry

    stored(frames, [steps * p // parts for p in range(parts + 1)], held, out, sems, tile)


def swaps(n):
    even = [min(i ^ 1, n - 1) for i in range(n)]
    odd = [min(max(((i - 1) ^ 1) + 1, 0), n - 1) for i in range(n)]
    return [list(enumerate(to)) for to in ((even, odd) if n > 2 else (even,))]


def sends(first, last, axis):
    is_even = lax.rem(lax.axis_index(axis), 2) == 0
    return jnp.where(is_even, last, first), jnp.where(is_even, first, last)


def halo_sends(hidden):
    rows, cols = hidden.shape[1:3]
    to_rows = sends(hidden[:, 0], hidden[:, rows - 1], ROW)
    return to_rows, sends(hidden[:, :, 0], hidden[:, :, cols - 1], "col")


def with_corners(to_rows, by_cols):
    frames, cols, channels = to_rows[0].shape
    n_cols = lax.axis_size("col")
    if n_cols == 1:
        return to_rows
    sides = by_cols[:1] if n_cols == 2 else chosen(*by_cols, *place("col"))
    wide = -(-channels // (cols * LANE)) * LANE
    packed = []
    for side in sides:
        corners = sends(side[:, 0], side[:, side.shape[1] - 1], ROW)
        spare = ((0, 0), (0, cols * wide - channels))
        packed.append([jnp.pad(x, spare).reshape(frames, cols, wide) for x in corners])
    return [jnp.concatenate(parts, axis=2) for parts in zip(to_rows, *packed)]


def both(results):
    return [results[0], results[-1]]


def swap_even_rows(to_even):
    return lax.ppermute(to_even, ROW, swaps(lax.axis_size(ROW))[0])


def swap_odd_rows(to_odd):
    pairs = swaps(lax.axis_size(ROW))[1:]
    return lax.ppermute(to_odd, ROW, pairs[0]) if pairs else to_odd


def swap_columns(to_cols):
    pairs = swaps(lax.axis_size("col"))
    return both([lax.ppermute(x, "col", p) for x, p in zip(to_cols, pairs)])


def convolve(kernel, name, result, *arrays):
    return pl.pallas_call(
        kernel,
        out_shape=result,
        in_specs=whole(len(arrays)),
        out_specs=pl.BlockSpec(memory_space=pl.ANY),
        scratch_shapes=[
            pltpu.VMEM(result.shape, result.dtype),
            pltpu.SemaphoreType.DMA((2, result.shape[0])),
        ],
        compiler_params=pltpu.CompilerParams(vmem_limit_bytes=VMEM_LIMIT),
        cost_estimate=pl.CostEstimate(
            flops=20 * result.size, bytes_accessed=6 * result.size, transcendentals=0
        ),
        name=name,
    )(*arrays)


ROW = ("row_far", "row_near")
GROUP = ("row_near", "col")


def across(value):
    n = lax.axis_size("row_far")
    return [
        lax.ppermute(value, "row_far", [(i, (i + step) % n) for i in range(n)])
        for step in range(1, n)
    ]


def exchange(value, step):
    n = lax.axis_size(GROUP)
    return lax.ppermute(value, GROUP, [(i, target(i, step, n)) for i in range(n)])


def frame_prefix(value):
    n, mine = lax.axis_size("frame"), lax.axis_index("frame")
    running = value
    doubling = n & (n - 1) == 0
    step = 1
    while step < n:
        pairs = [(i, i ^ step if doubling else (i + step) % n) for i in range(n)]
        got = lax.ppermute(value, "frame", pairs)
        running = running + jnp.where(mine & step != 0 if doubling else mine >= step, got, 0)
        value = value + got if doubling else value
        step = 2 * step if doubling else step + 1
    return running


def on_device(queries, keys, values, hidden, conv_weight, conv_bias):
    width = queries.shape[-1]
    tokens = queries.size // width
    pieces = lax.axis_size(GROUP)
    per = piece_rows(width, pieces)

    local = pl.pallas_call(
        functools.partial(state_kernel, width, pieces),
        out_shape=[jax.ShapeDtypeStruct((per // 8, 8, LANE), F32)] * pieces,
        in_specs=[pl.BlockSpec(memory_space=pltpu.HBM)] * 2,
        out_specs=whole(pieces),
        scratch_shapes=[
            pltpu.VMEM((tokens, width), BF16),
            pltpu.VMEM((tokens, width), BF16),
            pltpu.VMEM((pieces * per, LANE), F32),
            pltpu.SemaphoreType.DMA((2, 2)),
        ],
        compiler_params=pltpu.CompilerParams(vmem_limit_bytes=VMEM_MOST),
        cost_estimate=pl.CostEstimate(
            flops=2 * tokens * width * HD, bytes_accessed=6 * tokens * width, transcendentals=0
        ),
        name="local_state",
    )(keys.reshape(tokens, width), values.reshape(tokens, width))

    near = sum((exchange(local[step], step) for step in range(pieces - 1, 0, -1)), local[0])
    near, (to_rows, to_cols), bias = lax.optimization_barrier(
        (near, halo_sends(hidden), conv_bias)
    )
    summed = jax.ShapeDtypeStruct(hidden.shape, F32)
    inner = convolve(
        inner_kernel, "conv_inner", summed, hidden, conv_weight, bias.reshape(-1, LANE)
    )
    block, by_cols, to_rows, inner = lax.optimization_barrier(
        (sum(across(near), near), swap_columns(to_cols), to_rows, inner)
    )

    to_even, to_odd = with_corners(to_rows, by_cols)
    prefix = frame_prefix(block)
    by_rows = swap_even_rows(to_even), swap_odd_rows(to_odd)
    others = [exchange(prefix, step) for step in range(pieces - 1, 0, -1)]
    halos = (*by_rows[::-1], *by_cols)
    result = jax.ShapeDtypeStruct((*hidden.shape[:3], hidden.shape[3] // 2), BF16)
    gated = convolve(outer_kernel, "conv_gate", result, inner, *halos, conv_weight)
    others, gated = lax.optimization_barrier((others, gated))
    attended = pl.pallas_call(
        functools.partial(attend_kernel, width),
        out_shape=jax.ShapeDtypeStruct((tokens, width), BF16),
        in_specs=whole(1 + pieces),
        out_specs=pl.BlockSpec(memory_space=pl.ANY),
        scratch_shapes=[
            pltpu.VMEM((pieces * per, LANE), F32),
            pltpu.VMEM((tokens, width), BF16),
            pltpu.SemaphoreType.DMA((3,)),
        ],
        compiler_params=pltpu.CompilerParams(vmem_limit_bytes=VMEM_LIMIT),
        cost_estimate=pl.CostEstimate(
            flops=8 * tokens * width * HD, bytes_accessed=6 * tokens * width, transcendentals=0
        ),
        name="attend",
    )(queries.reshape(tokens, width), *others, prefix)
    return attended.reshape(queries.shape), gated


def solution(mesh):
    frame, row, col = (mesh.shape[name] for name in ("frame", "row", "col"))
    near = 2 if row % 2 == 0 else 1
    split = jax.sharding.Mesh(
        mesh.devices.reshape(frame, row // near, near, col), ("frame", *ROW, "col")
    )
    placed = P("frame", ROW, "col", None)
    return jax.shard_map(
        on_device,
        mesh=split,
        in_specs=(placed, placed, placed, placed, P(), P()),
        out_specs=(placed, placed),
        check_vma=False,
    )
```
